256 devices in a mesh: pp: 8 (over y, x_hi), ep: 32 (over z, x_lo, core).
Axes of the slice: x: 4 (x_hi: 2, x_lo: 2; x = x_hi * 2 + x_lo), y: 4, z: 8, core: 2. Of those that a mesh axis runs over, the one named last changes fastest.
Arguments:
- forward_in: bfloat16 [8, 4096, 7168], P('pp', 'ep'), may hold values from -4 to 4
- grad_in: bfloat16 [8, 4096, 7168], P('pp', 'ep'), may hold values from -4 to 4
- routes: int32 [8, 2, 2, 4096, 8], P('pp', None, None, 'ep'), may hold values from 0 to 255, as said below
- gate_weights: float32 [8, 2, 2, 4096, 8], P('pp', None, None, 'ep'), may hold values from 0.1 to 1
- saved_preact: bfloat16 [8, 2, 32, 32, 5, 256], P('pp', None, 'ep'), may hold values from -6 to 6
- gate_up: bfloat16 [8, 32, 7168, 256], P('pp', 'ep'), may hold values from -0.0625 to 0.0625
- down_proj: bfloat16 [8, 32, 128, 7168], P('pp', 'ep'), may hold values from -0.125 to 0.125
Outputs:
- forward_out: bfloat16 [8, 4096, 7168], P('pp', 'ep')
- grad_out: bfloat16 [8, 4096, 7168], P('pp', 'ep')
The draws below stay inside these ranges and needn't reach their ends.
Inputs may be any that keep to these rules, and one draw needn't show every extreme that they name: `routes`: each row names 8 different experts. In each aligned block of 128 rows (the rows of one device), each expert below 2 is named by 2 to 5 rows; for every section, segment and stream one of these experts is named by exactly 5 rows in every block, and each of them by exactly 5 rows in at least one block.
All inputs are finite; a program needn't handle non-finite values.
Results may differ from the reference program's by a relative error of at most 0.0034.
Values may be sent and summed in bfloat16 or wider, within the bound.
A program may use at most 128 MiB of HBM per device.

```python
import jax
import jax.numpy as jnp
from jax import lax

D = 7168
HID = 2048
EXPERTS = 256
TOPK = 8
EXP_SEC = 2
SEGMENTS = 2
TOK_DEV = 128
TOKENS = 4096
HID_DEV = 128
CAP = 5
N_PP = 8
N_EP = 32


def draw_routes(key, part):
    groups = N_PP * SEGMENTS * 2
    keys = jax.random.split(key, 6)
    others = EXPERTS - EXP_SEC
    noise = jax.random.randint(keys[0], (groups, TOKENS, others), 0, 2 ** 20)
    distinct = noise * EXPERTS + jnp.arange(others, dtype=jnp.int32)[None, None, :]
    chosen = lax.top_k(distinct, TOPK)[1].astype(jnp.int32) + EXP_SEC
    counts = jax.random.randint(keys[1], (groups, N_EP, EXP_SEC), 2, CAP + 1)
    full_expert = jax.random.randint(keys[2], (groups, 1, 1), 0, EXP_SEC)
    counts = jnp.where(jnp.arange(EXP_SEC, dtype=jnp.int32)[None, None, :] == full_expert, CAP, counts)
    block_pick = jax.random.randint(keys[3], (groups, 1, 1), 0, N_EP)
    counts = jnp.where(jnp.arange(N_EP, dtype=jnp.int32)[None, :, None] == block_pick, CAP, counts)
    ordering = jax.random.randint(keys[4], (groups, N_EP, TOK_DEV, EXP_SEC), 0, 2 ** 16) * TOK_DEV
    ordering = ordering + jnp.arange(TOK_DEV, dtype=jnp.int32)[None, None, :, None]
    position = jnp.argsort(jnp.argsort(ordering, axis=2), axis=2)
    member = (position < counts[:, :, None, :]).reshape(groups, TOKENS, EXP_SEC)
    slot_noise = jax.random.randint(keys[5], (groups, TOKENS, TOPK), 0, 2 ** 16) * TOPK
    slot_order = jnp.argsort(slot_noise + jnp.arange(TOPK, dtype=jnp.int32)[None, None, :], axis=2)
    result = chosen
    for expert in range(EXP_SEC):
        place_hit = jnp.arange(TOPK, dtype=jnp.int32)[None, None, :] == slot_order[:, :, expert:expert + 1]
        place_hit = place_hit & member[:, :, expert:expert + 1]
        result = jnp.where(place_hit, expert, result)
    return result.reshape(N_PP, SEGMENTS, 2, TOKENS, TOPK).astype(jnp.int32)


def shard_levels(own_key, dims, cuts, least, high):
    def one(axis_at, parts):
        heights = jax.random.uniform(jax.random.fold_in(jax.random.fold_in(own_key, 6), axis_at), (parts,), jnp.float32, least / len(cuts), high / len(cuts))
        return jnp.repeat(jnp.exp(heights), dims[axis_at] // parts).reshape((-1,) + (1,) * (len(dims) - axis_at - 1))

    loudness = one(*cuts[0])
    for cut in cuts[1:]:
        loudness = loudness * one(*cut)
    return loudness


def centred(stream_key, shape, deviation, bound, cuts=(), held_as=jnp.bfloat16):
    values = deviation * jax.random.normal(stream_key, shape, jnp.float32)
    if cuts:
        values = values * shard_levels(stream_key, shape, cuts, -0.22, 0.18)
    return jnp.clip(values, -bound, bound).astype(held_as)


def setup_inputs(seed: int = 0) -> dict:
    key_list = jax.random.split(jax.random.key(seed), 8)
    forward_in = centred(key_list[0], (N_PP, TOKENS, D), 0.5, 4.0, ((0, 8), (1, 32)))
    grad_in = centred(key_list[1], (N_PP, TOKENS, D), 0.5, 4.0, ((0, 8), (1, 32)))
    routes = draw_routes(jax.random.fold_in(key_list[7], 71), 0)
    gate_weights = jnp.clip(0.1 + 0.9 * jax.random.uniform(key_list[3], (N_PP, SEGMENTS, 2, TOKENS, TOPK), jnp.float32) ** shard_levels(key_list[3], (N_PP, SEGMENTS, 2, TOKENS, TOPK), ((0, 8), (3, 32)), -0.2, 0.2), 0.1, 1.0)
    saved_preact = centred(key_list[4], (N_PP, SEGMENTS, N_EP, N_EP, CAP, 2 * HID_DEV), 1.0, 6.0, ((0, 8), (2, 32)))
    gate_up = centred(key_list[5], (N_PP, N_EP, D, 2 * HID_DEV), D ** -0.5, 0.0625, ((0, 8), (1, 32)))
    down_proj = centred(key_list[6], (N_PP, N_EP, HID_DEV, D), HID ** -0.5, 0.125, ((0, 8), (1, 32)))
    return {"forward_in": forward_in, "grad_in": grad_in, "routes": routes, "gate_weights": gate_weights, "saved_preact": saved_preact, "gate_up": gate_up, "down_proj": down_proj}


def slot_tables(expert_ids, weights, experts_here, capacity):
    labels = jnp.arange(experts_here, dtype=jnp.int32)
    is_named = expert_ids[:, :, None] == labels[None, None, :]
    member = jnp.any(is_named, axis=1)
    scales = jnp.sum(jnp.where(is_named, weights[:, :, None], jnp.zeros_like(weights[:, :, None])), axis=1)
    slot_rank = jnp.cumsum(member.astype(jnp.int32), axis=0) - 1
    places = jnp.arange(capacity, dtype=jnp.int32)
    onehot = member[:, :, None] & (slot_rank[:, :, None] == places[None, None, :])
    return onehot, scales


def spread_rows(onehot, scales, totals, inputs):
    combine = (onehot.astype(jnp.float32) * scales[:, :, None]).reshape(onehot.shape[0], -1)
    flat_totals = totals.reshape(combine.shape[1], -1)
    summed = jnp.dot(combine, flat_totals, precision=lax.Precision.HIGHEST, preferred_element_type=jnp.float32)
    return (summed + inputs.astype(jnp.float32)).astype(jnp.bfloat16)


def expert_forward(routed, w_in, w_out):
    sources, capacity, model_width = routed.shape
    flat_rows = routed.reshape(sources * capacity, model_width)
    hidden_width = w_out.shape[0]
    activation = jnp.dot(flat_rows, w_in, preferred_element_type=jnp.float32)
    hidden = (jax.nn.silu(activation[:, :hidden_width]) * activation[:, hidden_width:]).astype(jnp.bfloat16)
    result = jnp.dot(hidden, w_out, preferred_element_type=jnp.float32).astype(jnp.bfloat16)
    return result.reshape(sources, capacity, model_width)


def expert_backward(routed, stored, w_in, w_out):
    sources, capacity, model_width = routed.shape
    flat_rows = routed.reshape(sources * capacity, model_width)
    hidden_width = w_out.shape[0]
    preact = stored.reshape(sources * capacity, 2 * hidden_width).astype(jnp.float32)
    gate_pre = preact[:, :hidden_width]
    up_pre = preact[:, hidden_width:]
    grad_hidden = lax.dot_general(flat_rows, w_out, (((1,), (1,)), ((), ())), preferred_element_type=jnp.float32)
    sigmoid_gate = jax.nn.sigmoid(gate_pre)
    grad_gate = grad_hidden * up_pre * sigmoid_gate * (1.0 + gate_pre * (1.0 - sigmoid_gate))
    grad_up = grad_hidden * gate_pre * sigmoid_gate
    grad_pair = jnp.concatenate([grad_gate, grad_up], axis=1).astype(jnp.bfloat16)
    returned = lax.dot_general(grad_pair, w_in, (((1,), (1,)), ((), ())), preferred_element_type=jnp.float32)
    return returned.astype(jnp.bfloat16).reshape(sources, capacity, model_width)


def run_section(tokens, expert_ids, weights, w_in_all, w_out_all, stored_all):
    split_ways = N_EP // EXP_SEC
    blocks = tokens.reshape(N_EP, TOK_DEV, D)
    onehot, scales = jax.vmap(lambda ident, weight_rows: slot_tables(ident, weight_rows, EXP_SEC, CAP))(
        expert_ids.reshape(N_EP, TOK_DEV, TOPK), weights.reshape(N_EP, TOK_DEV, TOPK))
    packed = jnp.einsum("jtec,jtd->jecd", onehot.astype(jnp.float32), blocks.astype(jnp.float32)).astype(jnp.bfloat16)
    shard_ids = jnp.arange(N_EP, dtype=jnp.int32)
    if stored_all is None:
        def shard_work(operands):
            shard_index, w_in, w_out = operands
            routed = lax.dynamic_index_in_dim(packed, shard_index // split_ways, axis=1, keepdims=False)
            return expert_forward(routed, w_in, w_out)
        partials = lax.map(shard_work, (shard_ids, w_in_all, w_out_all))
    else:
        def shard_work(operands):
            shard_index, w_in, w_out, stored = operands
            routed = lax.dynamic_index_in_dim(packed, shard_index // split_ways, axis=1, keepdims=False)
            return expert_backward(routed, stored, w_in, w_out)
        partials = lax.map(shard_work, (shard_ids, w_in_all, w_out_all, stored_all))
    totals = jnp.sum(partials.astype(jnp.float32).reshape(EXP_SEC, split_ways, N_EP, CAP, D), axis=1)
    totals = jnp.transpose(totals, (1, 0, 2, 3))
    result = jax.vmap(spread_rows)(onehot, scales, totals, blocks)
    return result.reshape(TOKENS, D)


def reference(forward_in, grad_in, routes, gate_weights, saved_preact, gate_up, down_proj):
    moving = forward_in
    falling = grad_in
    for step_index in range(SEGMENTS):
        moving = jnp.roll(moving, 1, axis=0)
        falling = jnp.roll(falling, -1, axis=0)
        next_moving = []
        next_falling = []
        for section in range(N_PP):
            next_moving.append(run_section(moving[section], routes[section, step_index, 0],
                                           gate_weights[section, step_index, 0], gate_up[section],
                                           down_proj[section], None))
            next_falling.append(run_section(falling[section], routes[section, step_index, 1],
                                            gate_weights[section, step_index, 1], gate_up[section],
                                            down_proj[section], saved_preact[section, step_index]))
        moving = jnp.stack(next_moving)
        falling = jnp.stack(next_falling)
    return moving, falling
```

```python
import functools

import jax
import jax.numpy as jnp
from jax import lax
from jax.experimental import pallas as pl
from jax.experimental.pallas import tpu as pltpu
from jax.sharding import PartitionSpec as P

EXP_SEC = 2
SEGMENTS = 2
CAP = 5
MESH = pl.DeviceIdType.MESH

HALF = 3584
LANES = 1280
PARTS = ((0, 1280), (1280, 1152), (2432, 1152))
PART_ROWS = ((0, 1, 2, 3, 4), (8, 9, 10, 11, 12), (5, 6, 7, 13, 14))
STEP = 256
NZ = 8


def fold(t):
    rows, n = t.shape
    t = t.reshape(rows // 16, 16, n)
    a = t[:, :8].reshape(rows // 2, n)
    b = t[:, 8:].reshape(rows // 2, n)
    r = lax.rem(lax.broadcasted_iota(jnp.int32, (rows // 2, 1), 0), 8)
    size = rows // 2
    low = jnp.where(r < 3, pltpu.roll(a, size - 5, 0), pltpu.roll(b, size - 2, 0))
    return jnp.where(r < CAP, a + b + low, 0.0)


def expand(h):
    rows, n = h.shape
    r = lax.rem(lax.broadcasted_iota(jnp.int32, (rows, 1), 0), 8)
    first = jnp.where(r < CAP, h, 0.0)
    third_a = jnp.where(r >= 5, pltpu.roll(h, 5, 0), 0.0)
    third_b = jnp.where((r == 5) | (r == 6), pltpu.roll(h, 2, 0), 0.0)
    none = jnp.zeros_like(first)

    def both(a, b):
        a, b = a.reshape(rows // 8, 8, n), b.reshape(rows // 8, 8, n)
        return jnp.concatenate([a, b], axis=1).reshape(rows * 2, n).astype(jnp.bfloat16)

    return both(first, none), both(none, first), both(third_a, third_b)


def pick(products):
    rows = products[0].shape[0]
    r = lax.rem(lax.broadcasted_iota(jnp.int32, (rows, 1), 0), 16)
    second = (r >= 8) & (r < 13)
    third = ((r >= 5) & (r < 8)) | (r >= 13)
    return jnp.where(second, products[1], jnp.where(third, products[2], products[0]))


def nt(a, b):
    return lax.dot_general(a, b, (((1,), (1,)), ((), ())), preferred_element_type=jnp.float32)


def nn(a, b):
    return jnp.dot(a, b, preferred_element_type=jnp.float32)


def stage_kernel(packed, stored, w_in, w_out, out, src, gat, win, wout, spx, preo_a, pret_a, preo_b, pret_b, obuf, xr,
                 own, zb, rz, fin, tb, lsem, wss, wrs, twss, twrs, gss, grs, xss, xrs, oss, ors, zss, zrs):
    me = lax.axis_index("ep")
    z = me // 4
    x = lax.rem(me // 2, 2)
    c = lax.rem(me, 2)
    other = 1 - c
    twin = z * 4 + x * 2 + other
    across = z * 4 + (1 - x) * 2 + c

    def at_z(zz):
        return zz * 4 + x * 2 + c

    def remote(a, b, ss, rs, device):
        return pltpu.make_async_remote_copy(
            src_ref=a, dst_ref=b, send_sem=ss, recv_sem=rs, device_id={"ep": device}, device_id_type=MESH)

    barrier = pltpu.get_barrier_semaphore()
    for device in [twin, across] + [at_z(lax.rem(z + d, NZ)) for d in range(1, NZ)]:
        pl.semaphore_signal(barrier, inc=1, device_id={"ep": device}, device_id_type=MESH)
    pl.semaphore_wait(barrier, 2 + NZ - 1)

    started = []
    pack_copies = []
    for s in range(2):
        copy = remote(packed.at[s, :, other], src.at[s, :, c], twss.at[s], twrs.at[s], twin)
        copy.start()
        pack_copies.append(copy)
        src[s, :, c] = packed[s, :, c]
    started += pack_copies

    weight_copies = []
    local_copies = []
    for p, (off, width) in enumerate(PARTS):
        mine = pl.multiple_of(c * HALF + off, 128)
        theirs = pl.multiple_of(other * HALF + off, 128)
        inner = pl.ds(p * LANES, width)
        down = pl.ds(pl.multiple_of(c * 128, 128), 128)
        pairs = (
            (w_in.at[pl.ds(mine, width)], w_in.at[pl.ds(theirs, width)], win.at[c, inner]),
            (w_out.at[:, pl.ds(mine, width)], w_out.at[:, pl.ds(theirs, width)], wout.at[down, inner]),
        )
        for k, (keep, give, slot) in enumerate(pairs):
            copy = remote(give, slot, wss.at[2 * p + k], wrs.at[2 * p + k], twin)
            copy.start()
            weight_copies.append(copy)
            copy = pltpu.make_async_copy(keep, slot, lsem.at[2 * p + k])
            copy.start()
            local_copies.append(copy)
        if width < LANES:
            win[:, p * LANES + width:(p + 1) * LANES] = jnp.zeros((2, LANES - width, 256), jnp.bfloat16)
            wout[:, p * LANES + width:(p + 1) * LANES] = jnp.zeros((256, LANES - width), jnp.bfloat16)
    copy = remote(stored, spx.at[c], wss.at[6], wrs.at[6], twin)
    copy.start()
    weight_copies.append(copy)
    spx[c] = stored[...]

    z_copies = [[], []]
    for s in range(2):
        pack_copies[s].wait_recv()
        for d in (1, 7, 2, 6, 3, 5, 4):
            to = lax.rem(z + d, NZ)
            copy = remote(src.at[s, to // 4], gat.at[s, x, z], gss.at[s, d], grs.at[s, d], at_z(to))
            copy.start()
            z_copies[s].append((d, copy))
        gat[s, x, z] = src[s, z // 4]

    x_copies = [[], []]

    def relay(s):
        copy = remote(gat.at[s, x, z], gat.at[s, x, z], xss.at[s, 0], xrs.at[s, 0], across)
        copy.start()
        x_copies[s].append(copy)
        for d, arriving in z_copies[s]:
            arriving.wait_recv()
            back = lax.rem(z + NZ - d, NZ)
            copy = remote(gat.at[s, x, back], gat.at[s, x, back], xss.at[s, d], xrs.at[s, d], across)
            copy.start()
            x_copies[s].append(copy)

    def pre(s, line):
        rows = gat[s, line].reshape(NZ * 32, LANES)
        if s == 0:
            for k in range(2):
                t = pick([nn(rows, win[k, p * LANES:(p + 1) * LANES]) for p in range(3)])
                preo_a[line, :, k * 256:(k + 1) * 256] = fold(t)
        else:
            t = pick([nt(rows, wout[:, p * LANES:(p + 1) * LANES]) for p in range(3)])
            preo_b[line] = fold(t)

    def swap_pre(s):
        mine, theirs = ((preo_a, pret_a), (preo_b, pret_b))[s]
        copy = remote(mine, theirs, twss.at[2 + s], twrs.at[2 + s], twin)
        copy.start()
        started.append(copy)
        return copy

    def hidden(s, line):
        if s == 0:
            g = preo_a[line] + pret_a[line]
            return jnp.concatenate([
                jax.nn.silu(g[:, 256 * k:256 * k + 128]) * g[:, 256 * k + 128:256 * k + 256] for k in range(2)], axis=1)
        g = preo_b[line] + pret_b[line]
        cols = []
        for k in range(2):
            ab = spx[k, line].astype(jnp.float32)
            a, b = ab[:, :128], ab[:, 128:]
            q = jax.nn.sigmoid(a)
            gk = g[:, 128 * k:128 * k + 128]
            cols += [gk * b * q * (1.0 + a * (1.0 - q)), gk * a * q]
        return jnp.concatenate(cols, axis=1)

    def post(s, line, emit):
        parts = expand(hidden(s, line))

        @pl.loop(0, LANES // STEP)
        def _(n):
            total = None
            for p in range(3):
                cols = pl.ds(pl.multiple_of(p * LANES + n * STEP, STEP), STEP)
                if s == 0:
                    terms = [nn(parts[p], wout[:, cols])]
                else:
                    terms = [nt(parts[p][:, 256 * k:256 * k + 256], win[k, cols]) for k in range(2)]
                for term in terms:
                    total = term if total is None else total + term
            emit(n, total)

    def chunk(s, n):
        cols = pl.ds(pl.multiple_of(n * STEP, STEP), STEP)
        return remote(obuf.at[s, :, cols], xr.at[s, :, cols], oss.at[s, n], ors.at[s, n], across)

    def give_across(s):
        def emit(n, total):
            obuf[s, :, pl.ds(pl.multiple_of(n * STEP, STEP), STEP)] = total.astype(jnp.bfloat16)
            chunk(s, n).start()

        post(s, 1 - x, emit)

    def keep(s):
        def emit(n, total):
            own[s, :, pl.ds(pl.multiple_of(n * STEP, STEP), STEP)] = total

        post(s, x, emit)

    back_copies = [[], []]

    def give_back(s):
        @pl.loop(0, LANES // STEP)
        def _(n):
            cols = pl.ds(pl.multiple_of(n * STEP, STEP), STEP)
            chunk(s, n).wait_recv()
            total = own[s, :, cols] + xr[s, :, cols].astype(jnp.float32)
            zb[s, :, :, :, cols] = total.astype(jnp.bfloat16).reshape(NZ, 2, 16, STEP)

        for d in (4, 3, 5, 2, 6, 1, 7):
            to = lax.rem(z + d, NZ)
            copy = remote(zb.at[s, to], rz.at[s, z], zss.at[s, d], zrs.at[s, d], at_z(to))
            copy.start()
            back_copies[s].append(copy)
        rz[s, z] = zb[s, z]

    def finish(s):
        for copy in back_copies[s]:
            copy.wait_recv()
        for e in range(2):
            for core, slot in ((c, out.at[s, e, c]), (other, tb.at[s, e])):
                total = rz[s, 4 * e, core].astype(jnp.float32)
                for i in range(1, 4):
                    total = total + rz[s, 4 * e + i, core].astype(jnp.float32)
                slot[...] = total
        copy = remote(tb.at[s], fin.at[s], twss.at[4 + s], twrs.at[4 + s], twin)
        copy.start()
        started.append(copy)
        return copy

    def arrived(s):
        for copy in x_copies[s]:
            copy.wait_recv()

    relay(0)
    for copy in local_copies:
        copy.wait()
    for copy in weight_copies:
        copy.wait_recv()
    pre(0, x)
    relay(1)
    arrived(0)
    pre(0, 1 - x)
    swap_a = swap_pre(0)
    pre(1, x)
    swap_a.wait_recv()
    give_across(0)
    keep(0)
    arrived(1)
    pre(1, 1 - x)
    swap_b = swap_pre(1)
    give_back(0)
    swap_b.wait_recv()
    give_across(1)
    keep(1)
    give_back(1)
    last = [finish(0), finish(1)]
    for s in range(2):
        last[s].wait_recv()
        out[s, :, other] = fin[s]

    for copy in started + weight_copies:
        copy.wait_send()
    for s in range(2):
        for _, copy in z_copies[s]:
            copy.wait_send()
        for copy in x_copies[s] + back_copies[s]:
            copy.wait_send()

        @pl.loop(0, LANES // STEP)
        def _(n):
            chunk(s, n).wait_send()


def run_stage(packed, stored, w_in, w_out):
    bf16, f32 = jnp.bfloat16, jnp.float32
    vmem = pl.BlockSpec(memory_space=pltpu.VMEM)
    hbm = pl.BlockSpec(memory_space=pl.ANY)
    dma = pltpu.SemaphoreType.DMA
    return pl.pallas_call(
        stage_kernel,
        out_shape=jax.ShapeDtypeStruct((2, 2, 2, 16, LANES), f32),
        in_specs=[vmem, vmem, hbm, hbm],
        out_specs=vmem,
        scratch_shapes=[
            pltpu.VMEM((2, 2, 2, 16, LANES), bf16),
            pltpu.VMEM((2, 2, NZ, 2, 16, LANES), bf16),
            pltpu.VMEM((2, 3 * LANES, 256), bf16),
            pltpu.VMEM((256, 3 * LANES), bf16),
            pltpu.VMEM((2, 2, 128, 256), bf16),
            pltpu.VMEM((2, 128, 512), f32),
            pltpu.VMEM((2, 128, 512), f32),
            pltpu.VMEM((2, 128, 256), f32),
            pltpu.VMEM((2, 128, 256), f32),
            pltpu.VMEM((2, 256, LANES), bf16),
            pltpu.VMEM((2, 256, LANES), bf16),
            pltpu.VMEM((2, 256, LANES), f32),
            pltpu.VMEM((2, NZ, 2, 16, LANES), bf16),
            pltpu.VMEM((2, NZ, 2, 16, LANES), bf16),
            pltpu.VMEM((2, 2, 16, LANES), f32),
            pltpu.VMEM((2, 2, 16, LANES), f32),
            dma((6,)),
            dma((7,)), dma((7,)),
            dma((6,)), dma((6,)),
            dma((2, 8)), dma((2, 8)),
            dma((2, 8)), dma((2, 8)),
            dma((2, 5)), dma((2, 5)),
            dma((2, 8)), dma((2, 8)),
        ],
        compiler_params=pltpu.CompilerParams(
            collective_id=0, has_side_effects=True, vmem_limit_bytes=48 * 2 ** 20),
        name="expert_stage",
    )(packed, stored, w_in, w_out)


def passed_along(value, axis, steps):
    count = lax.axis_size(axis)
    pairs = [(source, (source + steps) % count) for source in range(count)]
    return lax.ppermute(value, axis, pairs)


def slot_tables(expert_ids, weights):
    labels = jnp.arange(EXP_SEC, dtype=jnp.int32)
    is_named = expert_ids[:, :, None] == labels[None, None, :]
    member = jnp.any(is_named, axis=1)
    scales = jnp.sum(jnp.where(is_named, weights[:, :, None], 0.0), axis=1)
    slot_rank = jnp.cumsum(member.astype(jnp.int32), axis=0) - 1
    places = jnp.arange(CAP, dtype=jnp.int32)
    onehot = member[:, :, None] & (slot_rank[:, :, None] == places[None, None, :])
    choose = jnp.transpose(onehot, (1, 2, 0)).reshape(EXP_SEC * CAP, -1)
    scaled = jnp.transpose(onehot * scales[:, :, None], (1, 2, 0)).reshape(EXP_SEC * CAP, -1)
    return choose.astype(jnp.float32), scaled


def to_tiles(rows):
    rows = rows.reshape(EXP_SEC, CAP, 2, HALF)
    pieces = [jnp.pad(rows[..., off:off + w], ((0, 0), (0, 0), (0, 0), (0, LANES - w))) for off, w in PARTS]
    pieces = [jnp.transpose(p, (0, 2, 1, 3)) for p in pieces]
    blank = jnp.zeros_like(pieces[0][:, :, :1])
    return jnp.concatenate([pieces[0], pieces[2][:, :, :3], pieces[1], pieces[2][:, :, 3:], blank], axis=2)


def from_tiles(tiles):
    pieces = [tiles[:, :, 0:5], tiles[:, :, 8:13], jnp.concatenate([tiles[:, :, 5:8], tiles[:, :, 13:15]], axis=2)]
    rows = jnp.concatenate([p[..., :w] for p, (_, w) in zip(pieces, PARTS)], axis=3)
    return jnp.transpose(rows, (0, 2, 1, 3)).reshape(EXP_SEC * CAP, 2 * HALF)


def choose_rows(choose, tokens):
    return jnp.dot(choose.astype(jnp.bfloat16), tokens, preferred_element_type=jnp.float32).astype(jnp.bfloat16)


def updated(rows, choose, scaled, tiles):
    mix = lax.dot_general(choose, scaled, (((1,), (1,)), ((), ())), precision=lax.Precision.HIGHEST)
    added = jnp.dot(mix, from_tiles(tiles), precision=lax.Precision.HIGHEST)
    return (rows.astype(jnp.float32) + added).astype(jnp.bfloat16)


def place(choose, rows, tokens):
    first = jnp.cumsum(choose, axis=0)
    lone = jnp.where(first == 1.0, choose, 0.0).astype(jnp.bfloat16)
    put = lax.dot_general(lone, rows, (((0,), (0,)), ((), ())), preferred_element_type=jnp.float32)
    touched = jnp.sum(choose, axis=0) > 0.0
    return jnp.where(touched[:, None], put.astype(jnp.bfloat16), tokens)


def local(forward_in, grad_in, routes, gate_weights, saved_preact, gate_up, down_proj):
    w_in = gate_up[0, 0]
    w_out = down_proj[0, 0]
    starts = (forward_in[0], grad_in[0])
    steps = (1, -1)
    tables = [[slot_tables(routes[0, t, s], gate_weights[0, t, s]) for s in range(2)] for t in range(2)]
    stored = jnp.transpose(saved_preact[0, :, 0].reshape(2, NZ, 2, 2, CAP, 256), (0, 2, 1, 3, 4, 5))
    stored = jnp.pad(stored, ((0, 0), (0, 0), (0, 0), (0, 0), (0, 8 - CAP), (0, 0))).reshape(2, 2, 128, 256)

    bulk = [passed_along(starts[s], "pp", 2 * steps[s]) for s in range(2)]
    rows = []
    for s in range(2):
        ahead = passed_along(tables[0][s][0].astype(jnp.bfloat16), "pp", -steps[s])
        rows.append(passed_along(choose_rows(ahead, starts[s]), "pp", steps[s]))
    sums = run_stage(jnp.stack([to_tiles(r) for r in rows]), stored[0], w_in, w_out)
    mids = []
    for s in range(2):
        choose, scaled = tables[0][s]
        fresh = passed_along(updated(rows[s], choose, scaled, sums[s]), "pp", steps[s])
        chosen = passed_along(choose.astype(jnp.bfloat16), "pp", steps[s])
        mids.append(place(chosen.astype(jnp.float32), fresh, bulk[s]))
    rows = [choose_rows(tables[1][s][0], mids[s]) for s in range(2)]
    sums = run_stage(jnp.stack([to_tiles(r) for r in rows]), stored[1], w_in, w_out)
    outs = []
    for s in range(2):
        choose, scaled = tables[1][s]
        outs.append(place(choose, updated(rows[s], choose, scaled, sums[s]), mids[s]))
    return (outs[0][None], outs[1][None])


def solution(mesh):
    in_specs = (
        P("pp", "ep", None),
        P("pp", "ep", None),
        P("pp", None, None, "ep", None),
        P("pp", None, None, "ep", None),
        P("pp", None, "ep", None, None, None),
        P("pp", "ep", None, None),
        P("pp", "ep", None, None),
    )
    out_specs = (P("pp", "ep", None), P("pp", "ep", None))
    return jax.shard_map(local, mesh=mesh, in_specs=in_specs, out_specs=out_specs, check_vma=False)
```

```python
import functools

import jax
import jax.numpy as jnp
from jax import lax
from jax.experimental import pallas as pl
from jax.experimental.pallas import tpu as pltpu
from jax.sharding import PartitionSpec as P

EXP_SEC = 2
SEGMENTS = 2
CAP = 5
MESH = pl.DeviceIdType.MESH

HALF = 3584
LANES = 1280
PARTS = ((0, 1280), (1280, 1152), (2432, 1152))
PART_ROWS = ((0, 1, 2, 3, 4), (8, 9, 10, 11, 12), (5, 6, 7, 13, 14))
STEP = 256
NZ = 8


def fold(t):
    rows, n = t.shape
    t = t.reshape(rows // 16, 16, n)
    a = t[:, :8].reshape(rows // 2, n)
    b = t[:, 8:].reshape(rows // 2, n)
    r = lax.rem(lax.broadcasted_iota(jnp.int32, (rows // 2, 1), 0), 8)
    size = rows // 2
    low = jnp.where(r < 3, pltpu.roll(a, size - 5, 0), pltpu.roll(b, size - 2, 0))
    return jnp.where(r < CAP, a + b + low, 0.0)


def expand(h, dtype=jnp.bfloat16):
    rows, n = h.shape
    r = lax.rem(lax.broadcasted_iota(jnp.int32, (rows, 1), 0), 8)
    first = jnp.where(r < CAP, h, 0.0)
    third_a = jnp.where(r >= 5, pltpu.roll(h, 5, 0), 0.0)
    third_b = jnp.where((r == 5) | (r == 6), pltpu.roll(h, 2, 0), 0.0)
    none = jnp.zeros_like(first)

    def both(a, b):
        a, b = a.reshape(rows // 8, 8, n), b.reshape(rows // 8, 8, n)
        return jnp.concatenate([a, b], axis=1).reshape(rows * 2, n).astype(dtype)

    return both(first, none), both(none, first), both(third_a, third_b)


def pick(products):
    rows = products[0].shape[0]
    r = lax.rem(lax.broadcasted_iota(jnp.int32, (rows, 1), 0), 16)
    second = (r >= 8) & (r < 13)
    third = ((r >= 5) & (r < 8)) | (r >= 13)
    return jnp.where(second, products[1], jnp.where(third, products[2], products[0]))


def nt(a, b):
    return lax.dot_general(a, b, (((1,), (1,)), ((), ())), preferred_element_type=jnp.float32)


def tn(a, b):
    return lax.dot_general(a, b, (((0,), (0,)), ((), ())), preferred_element_type=jnp.float32)


def nn(a, b):
    return jnp.dot(a, b, preferred_element_type=jnp.float32)


def tables(ids, weights=None):
    tokens = ids.shape[1]
    before = lax.broadcasted_iota(jnp.int32, (tokens, tokens), 0) <= lax.broadcasted_iota(jnp.int32, (tokens, tokens), 1)
    before = before.astype(jnp.float32).astype(jnp.bfloat16)
    place = lax.broadcasted_iota(jnp.int32, (8, tokens), 0).astype(jnp.float32)
    choose, scaled, lone, member = [], [], [], []
    for e in range(EXP_SEC):
        hit = ids == e
        named = jnp.sum(hit.astype(jnp.float32), axis=0, keepdims=True) + jnp.zeros((8, tokens), jnp.float32)
        rank = nn(named.astype(jnp.bfloat16), before)
        slot = jnp.where((named > 0.0) & (rank - 1.0 == place) & (place < CAP), 1.0, 0.0)
        choose.append(slot)
        lone.append(slot if e == 0 else slot * (1.0 - member[0]))
        member.append(named)
        if weights is not None:
            scaled.append(slot * jnp.sum(jnp.where(hit, weights, 0.0), axis=0, keepdims=True))
    choose, lone = jnp.concatenate(choose, axis=0), jnp.concatenate(lone, axis=0)
    scaled = jnp.concatenate(scaled, axis=0) if weights is not None else None
    touched = jnp.maximum(member[0], member[1])
    return choose, scaled, lone, touched


def pack(parts, tokens, half):
    wide = None
    for p, (off, width) in enumerate(PARTS):
        got = nn(parts[p], tokens[:, half * HALF + off:half * HALF + off + width])
        if width < LANES:
            got = jnp.concatenate([got, jnp.zeros((got.shape[0], LANES - width), jnp.float32)], axis=1)
        wide = got if wide is None else wide + got
    return wide


def relay_kernel(x_in, y_in, ids, weights, stored, w_in, w_out, out, xv, xb, rt0, rt2, idt, wtt, pk, src, gat, win, wout,
                 spx, preo_a, pret_a, preo_b, pret_b, obuf, xr, own, zb, rz, mt, nv, nw, base, lsem, wss, wrs, tss, trs,
                 pss, prs, bss, brs, twss, twrs, gss, grs, xss, xrs, oss, ors, zss, zrs):
    me = lax.axis_index("ep")
    pp = lax.axis_index("pp")
    n_pp = lax.axis_size("pp")
    z = me // 4
    x = lax.rem(me // 2, 2)
    c = lax.rem(me, 2)
    other = 1 - c
    twin = z * 4 + x * 2 + other
    across = z * 4 + (1 - x) * 2 + c
    steps = (1, n_pp - 1)
    bf16, f32 = jnp.bfloat16, jnp.float32

    def at_z(zz):
        return zz * 4 + x * 2 + c

    def remote(a, b, ss, rs, device, section=None):
        where = {"ep": device} if section is None else {"pp": section, "ep": device}
        return pltpu.make_async_remote_copy(
            src_ref=a, dst_ref=b, send_sem=ss, recv_sem=rs, device_id=where, device_id_type=MESH)

    def section(hops):
        return lax.rem(pp + hops, n_pp)

    partners = [{"ep": twin}, {"ep": across}] + [{"ep": at_z(lax.rem(z + d, NZ))} for d in range(1, NZ)]
    for hops in (1, n_pp - 1):
        partners += [{"pp": section(hops), "ep": me}, {"pp": section(hops), "ep": twin}]
    for hops in (2, n_pp - 2):
        partners.append({"pp": section(hops), "ep": me})
    locals_x = []
    for s, tokens in enumerate((x_in, y_in)):
        copy = pltpu.make_async_copy(tokens, xv.at[s], lsem.at[6 + s])
        copy.start()
        locals_x.append(copy)
    barrier = pltpu.get_barrier_semaphore()
    for device in partners:
        pl.semaphore_signal(barrier, inc=1, device_id=device, device_id_type=MESH)
    pl.semaphore_wait(barrier, len(partners))

    started = []

    def go(copy):
        copy.start()
        started.append(copy)
        return copy

    ahead, behind = [], []
    for s in range(2):
        ahead.append(go(remote(ids.at[0, s], rt0.at[s], tss.at[s, 0], trs.at[s, 0], me, section(n_pp - steps[s]))))
    for s in range(2):
        behind.append(go(remote(ids.at[0, s], rt2.at[s], tss.at[s, 1], trs.at[s, 1], me, section(steps[s]))))
    twin_tables = [go(remote(ids, idt, twss.at[0], twrs.at[0], twin)),
                   go(remote(weights, wtt, twss.at[1], twrs.at[1], twin))]

    weight_copies, local_copies = [], []
    for p, (off, width) in enumerate(PARTS):
        mine = pl.multiple_of(c * HALF + off, 128)
        theirs = pl.multiple_of(other * HALF + off, 128)
        inner = pl.ds(p * LANES, width)
        down = pl.ds(pl.multiple_of(c * 128, 128), 128)
        pairs = (
            (w_in.at[pl.ds(mine, width)], w_in.at[pl.ds(theirs, width)], win.at[c, inner]),
            (w_out.at[:, pl.ds(mine, width)], w_out.at[:, pl.ds(theirs, width)], wout.at[down, inner]),
        )
        for k, (keep_part, give_part, slot) in enumerate(pairs):
            weight_copies.append(go(remote(give_part, slot, wss.at[2 * p + k], wrs.at[2 * p + k], twin)))
            copy = pltpu.make_async_copy(keep_part, slot, lsem.at[2 * p + k])
            copy.start()
            local_copies.append(copy)
        if width < LANES:
            win[:, p * LANES + width:(p + 1) * LANES] = jnp.zeros((2, LANES - width, 256), bf16)
            wout[:, p * LANES + width:(p + 1) * LANES] = jnp.zeros((256, LANES - width), bf16)
    weight_copies.append(go(remote(stored, spx.at[c], wss.at[6], wrs.at[6], twin)))
    spx[c] = stored[...]

    first_rows = []
    for s in range(2):
        ahead[s].wait_recv()
        locals_x[s].wait()
        parts = expand(tables(rt0[s])[0])
        for half in range(2):
            pk[0, s, half] = pack(parts, xv.at[s], half).astype(bf16).reshape(2, 16, LANES)
        first_rows.append([
            go(remote(pk.at[0, s, half], src.at[0, s, :, c], pss.at[0, s, i], prs.at[0, s, i],
                      (me, twin)[i], section(steps[s])))
            for i, half in enumerate((c, other))])

    bulk = [go(remote(tokens, xb.at[s], bss.at[s], brs.at[s], me, section(2 * steps[s] if s == 0 else n_pp - 2)))
            for s, tokens in enumerate((x_in, y_in))]

    z_copies, x_copies, back_copies, swaps = {}, {}, {}, {}

    def dispatch(t, s):
        z_copies[t, s] = []
        for d in (1, 7, 2, 6, 3, 5, 4):
            to = lax.rem(z + d, NZ)
            copy = go(remote(src.at[t, s, to // 4], gat.at[t, s, x, z], gss.at[t, s, d], grs.at[t, s, d], at_z(to)))
            z_copies[t, s].append((d, copy))
        gat[t, s, x, z] = src[t, s, z // 4]

    def relay(t, s):
        def pass_on(block, d):
            slot = gat.at[t, s, x, block]
            return go(remote(slot, slot, xss.at[t, s, d], xrs.at[t, s, d], across))

        x_copies[t, s] = [pass_on(z, 0)]
        for d, arriving in z_copies[t, s]:
            arriving.wait_recv()
            x_copies[t, s].append(pass_on(lax.rem(z + NZ - d, NZ), d))

    def arrived(t, s):
        for copy in x_copies[t, s]:
            copy.wait_recv()

    def pre(t, s, line):
        rows = gat[t, s, line].reshape(NZ * 32, LANES)
        if s == 0:
            for k in range(2):
                got = pick([nn(rows, win[k, p * LANES:(p + 1) * LANES]) for p in range(3)])
                preo_a[t, line, :, k * 256:(k + 1) * 256] = fold(got)
        else:
            preo_b[t, line] = fold(pick([nt(rows, wout[:, p * LANES:(p + 1) * LANES]) for p in range(3)]))

    def swap(t, s):
        mine, theirs = ((preo_a, pret_a), (preo_b, pret_b))[s]
        i = 2 + 2 * t + s
        swaps[t, s] = go(remote(mine.at[t], theirs.at[t], twss.at[i], twrs.at[i], twin))

    def hidden(t, s, line):
        if s == 0:
            g = preo_a[t, line] + pret_a[t, line]
            return jnp.concatenate([
                jax.nn.silu(g[:, 256 * k:256 * k + 128]) * g[:, 256 * k + 128:256 * k + 256] for k in range(2)], axis=1)
        g = preo_b[t, line] + pret_b[t, line]
        cols = []
        for k in range(2):
            ab = spx[k, t, line].astype(f32)
            a, b = ab[:, :128], ab[:, 128:]
            q = jax.nn.sigmoid(a)
            gk = g[:, 128 * k:128 * k + 128]
            cols += [gk * b * q * (1.0 + a * (1.0 - q)), gk * a * q]
        return jnp.concatenate(cols, axis=1)

    def post(t, s, line, emit):
        parts = expand(hidden(t, s, line))

        @pl.loop(0, LANES // STEP)
        def _(n):
            total = None
            for p in range(3):
                cols = pl.ds(pl.multiple_of(p * LANES + n * STEP, STEP), STEP)
                if s == 0:
                    terms = [nn(parts[p], wout[:, cols])]
                else:
                    terms = [nt(parts[p][:, 256 * k:256 * k + 256], win[k, cols]) for k in range(2)]
                for term in terms:
                    total = term if total is None else total + term
            emit(n, total)

    def lanes(n):
        return pl.ds(pl.multiple_of(n * STEP, STEP), STEP)

    def chunk(t, s, n):
        return remote(obuf.at[t, s, :, lanes(n)], xr.at[t, s, :, lanes(n)], oss.at[t, s, n], ors.at[t, s, n], across)

    def give_across(t, s):
        swaps[t, s].wait_recv()

        def emit(n, total):
            obuf[t, s, :, lanes(n)] = total.astype(bf16)
            chunk(t, s, n).start()

        post(t, s, 1 - x, emit)

    def keep(t, s):
        def emit(n, total):
            own[s, :, lanes(n)] = total

        post(t, s, x, emit)

    def give_back(t, s):
        @pl.loop(0, LANES // STEP)
        def _(n):
            chunk(t, s, n).wait_recv()
            total = own[s, :, lanes(n)] + xr[t, s, :, lanes(n)].astype(f32)
            zb[t, s, :, :, :, lanes(n)] = total.astype(bf16).reshape(NZ, 2, 16, STEP)

        back_copies[t, s] = []
        for d in (4, 3, 5, 2, 6, 1, 7):
            to = lax.rem(z + d, NZ)
            back_copies[t, s].append(go(
                remote(zb.at[t, s, to], rz.at[t, s, z], zss.at[t, s, d], zrs.at[t, s, d], at_z(to))))
        rz[t, s, z] = zb[t, s, z]

    def finish(t, s):
        for copy in back_copies[t, s]:
            copy.wait_recv()
        for core in range(2):
            totals = []
            for e in range(2):
                total = rz[t, s, 4 * e, core].astype(f32)
                for i in range(1, 4):
                    total = total + rz[t, s, 4 * e + i, core].astype(f32)
                totals.append(total)
            added = jnp.dot(mt[t, s, core], jnp.concatenate(totals, axis=0), precision=lax.Precision.HIGHEST,
                            preferred_element_type=f32)
            fresh = src[t, s, :, core].reshape(32, LANES).astype(f32) + added
            nv[t, s, core] = fresh.astype(bf16).reshape(2, 16, LANES)

    def mixing():
        for copy in twin_tables:
            copy.wait_recv()
        for t in range(2):
            for s in range(2):
                for core, names, gains in ((c, ids, weights), (other, idt, wtt)):
                    choose, scaled, _, _ = tables(names[t, s], gains[t, s])
                    total = None
                    for a, b in zip(expand(choose, f32), expand(scaled, f32)):
                        term = lax.dot_general(a, b, (((1,), (1,)), ((), ())), precision=lax.Precision.HIGHEST,
                                               preferred_element_type=f32)
                        total = term if total is None else total + term
                    mt[t, s, core] = total

    def prepare(s):
        behind[s].wait_recv()
        bulk[s].wait_recv()
        touched = tables(rt2[s])[3][:1]
        parts = expand(tables(ids[1, s])[0] * (1.0 - touched))
        for half in range(2):
            base[s, half] = pack(parts, xb.at[s], half).astype(bf16)

    def pass_rows(s):
        return [go(remote(nv.at[0, s, core], nw.at[0, s, c], pss.at[1, s, i], prs.at[1, s, i], (me, twin)[i],
                          section(steps[s])))
                for i, core in enumerate((c, other))]

    def second_rows(s, arriving):
        for copy in arriving:
            copy.wait_recv()
        lone = expand(tables(rt2[s])[2])
        choose = expand(tables(ids[1, s])[0])
        mix = nt(choose[0], lone[0]) + nt(choose[1], lone[1]) + nt(choose[2], lone[2])
        mix = mix.astype(bf16)
        for half in range(2):
            rows = base[s, half].astype(f32) + nn(mix, nw[0, s, half].reshape(32, LANES))
            pk[1, s, half] = rows.astype(bf16).reshape(2, 16, LANES)
        copy = go(remote(pk.at[1, s, other], src.at[1, s, :, c], twss.at[6 + s], twrs.at[6 + s], twin))
        src[1, s, :, c] = pk[1, s, c]
        copy.wait_recv()

    def place(names, rows, old, new):
        _, _, lone, _ = tables(names)
        touched = tn(lone.astype(bf16), jnp.ones((16, 128), bf16))[:, :1] > 0.0
        parts = expand(lone)
        for half in range(2):
            for p, (off, width) in enumerate(PARTS):
                cols = slice(half * HALF + off, half * HALF + off + width)
                put = tn(parts[p], rows[half].reshape(32, LANES)[:, :width])
                new[:, cols] = jnp.where(touched, put, old[:, cols].astype(f32)).astype(bf16)

    def exchange_last(s):
        nw[1, s, c] = nv[1, s, c]
        return go(remote(nv.at[1, s, other], nw.at[1, s, c], twss.at[8 + s], twrs.at[8 + s], twin))

    for s in range(2):
        for copy in first_rows[s]:
            copy.wait_recv()
        dispatch(0, s)
    mixing()
    for t in range(2):
        relay(t, 0)
        if t == 0:
            for copy in local_copies:
                copy.wait()
            for copy in weight_copies:
                copy.wait_recv()
        pre(t, 0, x)
        relay(t, 1)
        arrived(t, 0)
        pre(t, 0, 1 - x)
        swap(t, 0)
        pre(t, 1, x)
        give_across(t, 0)
        keep(t, 0)
        arrived(t, 1)
        pre(t, 1, 1 - x)
        swap(t, 1)
        give_back(t, 0)
        give_across(t, 1)
        keep(t, 1)
        if t == 0:
            prepare(0)
        give_back(t, 1)
        if t == 0:
            prepare(1)
            finish(0, 0)
            passed = [pass_rows(0)]
            second_rows(0, passed[0])
            dispatch(1, 0)
            finish(0, 1)
            passed.append(pass_rows(1))
            second_rows(1, passed[1])
            dispatch(1, 1)
            for s in range(2):
                place(rt2[s], nw[0, s], xb.at[s], out.at[s])
        else:
            last = []
            for s in range(2):
                finish(1, s)
                last.append(exchange_last(s))
                if s == 0:
                    last[0].wait_recv()
                    place(ids[1, 0], nw[1, 0], out.at[0], out.at[0])
            last[1].wait_recv()
            place(ids[1, 1], nw[1, 1], out.at[1], out.at[1])

    for copy in started:
        copy.wait_send()
    for t in range(2):
        for s in range(2):
            @pl.loop(0, LANES // STEP)
            def _(n):
                chunk(t, s, n).wait_send()


def local(forward_in, grad_in, routes, gate_weights, saved_preact, gate_up, down_proj):
    bf16, f32 = jnp.bfloat16, jnp.float32
    tokens, width = forward_in.shape[1:]
    ids = jnp.transpose(routes[0], (0, 1, 3, 2))
    weights = jnp.transpose(gate_weights[0], (0, 1, 3, 2))
    stored = jnp.transpose(saved_preact[0, :, 0].reshape(2, NZ, 2, 2, CAP, 256), (0, 2, 1, 3, 4, 5))
    stored = jnp.pad(stored, ((0, 0), (0, 0), (0, 0), (0, 0), (0, 8 - CAP), (0, 0))).reshape(2, 2, 128, 256)
    vmem = pl.BlockSpec(memory_space=pltpu.VMEM)
    hbm = pl.BlockSpec(memory_space=pl.ANY)
    dma = pltpu.SemaphoreType.DMA
    out = pl.pallas_call(
        relay_kernel,
        out_shape=jax.ShapeDtypeStruct((2, tokens, width), bf16),
        in_specs=[hbm, hbm, vmem, vmem, vmem, hbm, hbm],
        out_specs=vmem,
        scratch_shapes=[
            pltpu.VMEM((2, tokens, width), bf16),
            pltpu.VMEM((2, tokens, width), bf16),
            pltpu.VMEM((2, 8, tokens), jnp.int32),
            pltpu.VMEM((2, 8, tokens), jnp.int32),
            pltpu.VMEM((2, 2, 8, tokens), jnp.int32),
            pltpu.VMEM((2, 2, 8, tokens), f32),
            pltpu.VMEM((2, 2, 2, 2, 16, LANES), bf16),
            pltpu.VMEM((2, 2, 2, 2, 16, LANES), bf16),
            pltpu.VMEM((2, 2, 2, NZ, 2, 16, LANES), bf16),
            pltpu.VMEM((2, 3 * LANES, 256), bf16),
            pltpu.VMEM((256, 3 * LANES), bf16),
            pltpu.VMEM((2, 2, 2, 128, 256), bf16),
            pltpu.VMEM((2, 2, 128, 512), f32),
            pltpu.VMEM((2, 2, 128, 512), f32),
            pltpu.VMEM((2, 2, 128, 256), f32),
            pltpu.VMEM((2, 2, 128, 256), f32),
            pltpu.VMEM((2, 2, 256, LANES), bf16),
            pltpu.VMEM((2, 2, 256, LANES), bf16),
            pltpu.VMEM((2, 256, LANES), f32),
            pltpu.VMEM((2, 2, NZ, 2, 16, LANES), bf16),
            pltpu.VMEM((2, 2, NZ, 2, 16, LANES), bf16),
            pltpu.VMEM((2, 2, 2, 32, 32), f32),
            pltpu.VMEM((2, 2, 2, 2, 16, LANES), bf16),
            pltpu.VMEM((2, 2, 2, 2, 16, LANES), bf16),
            pltpu.VMEM((2, 2, 32, LANES), bf16),
            dma((8,)),
            dma((7,)), dma((7,)),
            dma((2, 2)), dma((2, 2)),
            dma((2, 2, 2)), dma((2, 2, 2)),
            dma((2,)), dma((2,)),
            dma((10,)), dma((10,)),
            dma((2, 2, 8)), dma((2, 2, 8)),
            dma((2, 2, 8)), dma((2, 2, 8)),
            dma((2, 2, 5)), dma((2, 2, 5)),
            dma((2, 2, 8)), dma((2, 2, 8)),
        ],
        compiler_params=pltpu.CompilerParams(
            collective_id=0, has_side_effects=True, vmem_limit_bytes=56 * 2 ** 20),
        name="expert_relay",
    )(forward_in[0], grad_in[0], ids, weights, stored, gate_up[0, 0], down_proj[0, 0])
    return (out[0][None], out[1][None])


def solution(mesh):
    in_specs = (
        P("pp", "ep", None),
        P("pp", "ep", None),
        P("pp", None, None, "ep", None),
        P("pp", None, None, "ep", None),
        P("pp", None, "ep", None, None, None),
        P("pp", "ep", None, None),
        P("pp", "ep", None, None),
    )
    out_specs = (P("pp", "ep", None), P("pp", "ep", None))
    return jax.shard_map(local, mesh=mesh, in_specs=in_specs, out_specs=out_specs, check_vma=False)
```

```python
import functools

import jax
import jax.numpy as jnp
from jax import lax
from jax.experimental import pallas as pl
from jax.experimental.pallas import tpu as pltpu
from jax.sharding import PartitionSpec as P

EXP_SEC = 2
SEGMENTS = 2
CAP = 5
MESH = pl.DeviceIdType.MESH

HALF = 3584
LANES = 1152
REST = 3456
STEP = 384
NZ = 8


def row_in(rows, group):
    return lax.rem(lax.broadcasted_iota(jnp.int32, (rows, 1), 0), group)


def fold(parts, rests):
    rows, n = parts[0].shape
    size = rows // 2
    r = row_in(rows, 16)
    second = (r >= 8) & (r < 13)
    third = ((r >= 5) & (r < 8)) | (r >= 13)
    t = jnp.where(second, parts[1], jnp.where(third, parts[2], parts[0])).reshape(rows // 16, 16, n)
    a = t[:, :8].reshape(size, n)
    b = t[:, 8:].reshape(size, n)
    r = row_in(size, 8)
    low = jnp.where(r < 3, pltpu.roll(a, size - 5, 0), pltpu.roll(b, size - 2, 0))
    total = a + b + low
    for i, rest in enumerate(rests):
        rest = rest.reshape(rows // 16, 16, n)[:, 8:].reshape(size, n)
        total = total + jnp.where(r == i, pltpu.roll(rest, size - (7 - i), 0), 0.0)
    return jnp.where(r < CAP, total, 0.0)


def expand(h, dtype=jnp.bfloat16):
    rows, n = h.shape
    r = row_in(rows, 8)
    first = jnp.where(r < CAP, h, 0.0)
    third_a = jnp.where(r >= 5, pltpu.roll(h, 5, 0), 0.0)
    third_b = jnp.where((r == 5) | (r == 6), pltpu.roll(h, 2, 0), 0.0)
    none = jnp.zeros_like(first)

    def both(a, b):
        a, b = a.reshape(rows // 8, 8, n), b.reshape(rows // 8, 8, n)
        return jnp.concatenate([a, b], axis=1).reshape(rows * 2, n).astype(dtype)

    rests = [both(none, jnp.where(r == 7, pltpu.roll(h, 7 - i, 0), 0.0)) for i in range(CAP)]
    return [both(first, none), both(none, first), both(third_a, third_b)], rests


def nt(a, b):
    return lax.dot_general(a, b, (((1,), (1,)), ((), ())), preferred_element_type=jnp.float32)


def tn(a, b):
    return lax.dot_general(a, b, (((0,), (0,)), ((), ())), preferred_element_type=jnp.float32)


def nn(a, b):
    return jnp.dot(a, b, preferred_element_type=jnp.float32)


def tables(ids, weights=None):
    tokens = ids.shape[1]
    before = lax.broadcasted_iota(jnp.int32, (tokens, tokens), 0) <= lax.broadcasted_iota(jnp.int32, (tokens, tokens), 1)
    before = before.astype(jnp.float32).astype(jnp.bfloat16)
    place = lax.broadcasted_iota(jnp.int32, (8, tokens), 0).astype(jnp.float32)
    choose, scaled, lone, member = [], [], [], []
    for e in range(EXP_SEC):
        hit = ids == e
        named = jnp.sum(hit.astype(jnp.float32), axis=0, keepdims=True) + jnp.zeros((8, tokens), jnp.float32)
        rank = nn(named.astype(jnp.bfloat16), before)
        slot = jnp.where((named > 0.0) & (rank - 1.0 == place) & (place < CAP), 1.0, 0.0)
        choose.append(slot)
        lone.append(slot if e == 0 else slot * (1.0 - member[0]))
        member.append(named)
        if weights is not None:
            scaled.append(slot * jnp.sum(jnp.where(hit, weights, 0.0), axis=0, keepdims=True))
    choose, lone = jnp.concatenate(choose, axis=0), jnp.concatenate(lone, axis=0)
    scaled = jnp.concatenate(scaled, axis=0) if weights is not None else None
    touched = jnp.maximum(member[0], member[1])
    return choose, scaled, lone, touched


def part_cols(half, p):
    return slice(half * HALF + p * LANES, half * HALF + (p + 1) * LANES)


def rest_cols(half):
    return slice(half * HALF + REST, (half + 1) * HALF)


def in_lanes(rests):
    blank = jnp.zeros((rests[0].shape[0], LANES - 128 * CAP), jnp.float32)
    return jnp.concatenate(rests + [blank], axis=1)


def pack(choose, tokens, half):
    parts, rests = expand(choose)
    wide = in_lanes([nn(rest, tokens[:, rest_cols(half)]) for rest in rests])
    for p in range(3):
        wide = wide + nn(parts[p], tokens[:, part_cols(half, p)])
    return wide


def exact(a, b):
    return jnp.dot(a, b, precision=lax.Precision.HIGHEST, preferred_element_type=jnp.float32)


def mixer(left, right):
    def one(a, b):
        return lax.dot_general(a, b, (((1,), (1,)), ((), ())), precision=lax.Precision.HIGHEST,
                               preferred_element_type=jnp.float32)

    lefts, rights = expand(left, jnp.float32)[0], expand(right, jnp.float32)[0]
    return one(lefts[0], rights[0]) + one(lefts[1], rights[1]) + one(lefts[2], rights[2]), one(left, right)


def mixed(by_row, by_slot, rows):
    r = row_in(16, 8)
    last = jnp.concatenate([rows[8:16], rows[24:32]], axis=0)
    slots = jnp.zeros((16, 128), jnp.float32)
    for i in range(CAP):
        slots = jnp.where(r == i, pltpu.roll(last[:, 128 * i:128 * i + 128], 16 - (7 - i), 0), slots)
    slots = exact(by_slot, slots)
    none = jnp.zeros((8, 128), jnp.float32)
    rests = []
    for i in range(CAP):
        rest = jnp.where(r == 7, pltpu.roll(slots, 7 - i, 0), 0.0)
        rests.append(jnp.concatenate([none, rest[:8], none, rest[8:]], axis=0))
    return exact(by_row, rows) + in_lanes(rests)


def relay_kernel(x_in, y_in, ids, weights, stored, w_in, w_out, out0, out1, xv, xb, rt0, rt2, idt, wtt, pk, src, gat, win, wout,
                 spx, preo_a, pret_a, preo_b, pret_b, obuf, xr, own, zb, rz, mt, ms, nv, nw, base, lsem, wss, wrs, tss, trs,
                 pss, prs, bss, brs, twss, twrs, gss, grs, xss, xrs, oss, ors, zss, zrs):
    me = lax.axis_index("ep")
    pp = lax.axis_index("pp")
    n_pp = lax.axis_size("pp")
    z = me // 4
    x = lax.rem(me // 2, 2)
    c = lax.rem(me, 2)
    other = 1 - c
    twin = z * 4 + x * 2 + other
    across = z * 4 + (1 - x) * 2 + c
    steps = (1, n_pp - 1)
    bf16, f32 = jnp.bfloat16, jnp.float32

    def at_z(zz):
        return zz * 4 + x * 2 + c

    def remote(a, b, ss, rs, device, section=None):
        where = {"ep": device} if section is None else {"pp": section, "ep": device}
        return pltpu.make_async_remote_copy(
            src_ref=a, dst_ref=b, send_sem=ss, recv_sem=rs, device_id=where, device_id_type=MESH)

    def section(hops):
        return lax.rem(pp + hops, n_pp)

    partners = [{"ep": twin}, {"ep": across}] + [{"ep": at_z(lax.rem(z + d, NZ))} for d in range(1, NZ)]
    for hops in (1, n_pp - 1):
        partners += [{"pp": section(hops), "ep": me}, {"pp": section(hops), "ep": twin}]
    for hops in (2, n_pp - 2):
        partners.append({"pp": section(hops), "ep": me})
    locals_x = []
    for s, tokens in enumerate((x_in, y_in)):
        copy = pltpu.make_async_copy(tokens, xv.at[s], lsem.at[2 + s])
        copy.start()
        locals_x.append(copy)
    barrier = pltpu.get_barrier_semaphore()
    for device in partners:
        pl.semaphore_signal(barrier, inc=1, device_id=device, device_id_type=MESH)
    pl.semaphore_wait(barrier, len(partners))

    started = []

    def go(copy):
        copy.start()
        started.append(copy)
        return copy

    ahead, behind = [], []
    for s in range(2):
        ahead.append(go(remote(ids.at[0, s], rt0.at[s], tss.at[s, 0], trs.at[s, 0], me, section(n_pp - steps[s]))))
    for s in range(2):
        behind.append(go(remote(ids.at[0, s], rt2.at[s], tss.at[s, 1], trs.at[s, 1], me, section(steps[s]))))
    twin_tables = [go(remote(ids, idt, twss.at[0], twrs.at[0], twin)),
                   go(remote(weights, wtt, twss.at[1], twrs.at[1], twin))]

    weight_copies, local_copies = [], []
    mine = pl.ds(pl.multiple_of(c * HALF, 128), HALF)
    theirs = pl.ds(pl.multiple_of(other * HALF, 128), HALF)
    down = pl.ds(pl.multiple_of(c * 128, 128), 128)
    pairs = ((w_in.at[mine], w_in.at[theirs], win.at[c]), (w_out.at[:, mine], w_out.at[:, theirs], wout.at[down]))
    for k, (keep_part, give_part, slot) in enumerate(pairs):
        weight_copies.append(go(remote(give_part, slot, wss.at[k], wrs.at[k], twin)))
        copy = pltpu.make_async_copy(keep_part, slot, lsem.at[k])
        copy.start()
        local_copies.append(copy)
    weight_copies.append(go(remote(stored, spx.at[c], wss.at[2], wrs.at[2], twin)))
    spx[c] = stored[...]

    first_rows = []
    for s in range(2):
        ahead[s].wait_recv()
        locals_x[s].wait()
        choose = tables(rt0[s])[0]
        for half in range(2):
            pk[0, s, half] = pack(choose, xv.at[s], half).astype(bf16).reshape(2, 16, LANES)
        first_rows.append([
            go(remote(pk.at[0, s, half], src.at[0, s, :, c], pss.at[0, s, i], prs.at[0, s, i],
                      (me, twin)[i], section(steps[s])))
            for i, half in enumerate((c, other))])

    bulk = [go(remote(tokens, xb.at[s], bss.at[s], brs.at[s], me, section(2 * steps[s] if s == 0 else n_pp - 2)))
            for s, tokens in enumerate((x_in, y_in))]

    z_copies, x_copies, swaps = {}, {}, {}

    def dispatch(t, s):
        z_copies[t, s] = {}
        for d in (4, 3, 5, 2, 6, 1, 7):
            to = lax.rem(z + d, NZ)
            z_copies[t, s][d] = go(
                remote(src.at[t, s, to // 4], gat.at[t, s, x, z], gss.at[t, s, d], grs.at[t, s, d], at_z(to)))
        gat[t, s, x, z] = src[t, s, z // 4]

    def pass_across(t, s, d):
        slot = gat.at[t, s, x, lax.rem(z + NZ - d, NZ)]
        x_copies[t, s].append(go(remote(slot, slot, xss.at[t, s, d], xrs.at[t, s, d], across)))

    def relay_some(t, s, *hops):
        for d in hops:
            z_copies[t, s][d].wait_recv()
            pass_across(t, s, d)

    def relay_first(t, s):
        x_copies[t, s] = []
        pass_across(t, s, 0)
        relay_some(t, s, 3, 5)
        relay_some(t, s, 2, 6)

    def relay_last(t, s):
        relay_some(t, s, 1, 7, 4)

    def arrived(t, s):
        for copy in x_copies[t, s]:
            copy.wait_recv()

    def pre(t, s, line):
        rows = gat[t, s, line].reshape(NZ * 32, LANES)
        for k in range(2 - s):
            def product(lhs, cols):
                return nn(lhs, win[k, cols]) if s == 0 else nt(lhs, wout[:, cols])

            got = fold([product(rows, part_cols(0, p)) for p in range(3)],
                       [product(rows[:, 128 * i:128 * i + 128], rest_cols(0)) for i in range(CAP)])
            if s == 0:
                preo_a[t, line, :, k * 256:(k + 1) * 256] = got
            else:
                preo_b[t, line] = got

    def swap(t, s):
        mine, theirs = ((preo_a, pret_a), (preo_b, pret_b))[s]
        i = 2 + 2 * t + s
        swaps[t, s] = go(remote(mine.at[t], theirs.at[t], twss.at[i], twrs.at[i], twin))

    def hidden(t, s, line):
        if s == 0:
            g = preo_a[t, line] + pret_a[t, line]
            return jnp.concatenate([
                jax.nn.silu(g[:, 256 * k:256 * k + 128]) * g[:, 256 * k + 128:256 * k + 256] for k in range(2)], axis=1)
        g = preo_b[t, line] + pret_b[t, line]
        cols = []
        for k in range(2):
            ab = spx[k, t, line].astype(f32)
            a, b = ab[:, :128], ab[:, 128:]
            q = jax.nn.sigmoid(a)
            gk = g[:, 128 * k:128 * k + 128]
            cols += [gk * b * q * (1.0 + a * (1.0 - q)), gk * a * q]
        return jnp.concatenate(cols, axis=1)

    def post(t, s, line, emit):
        parts, rests = expand(hidden(t, s, line))

        def product(lhs, cols):
            if s == 0:
                return nn(lhs, wout[:, cols])
            return nt(lhs[:, :256], win[0, cols]) + nt(lhs[:, 256:], win[1, cols])

        for n in range(LANES // STEP):
            total = None
            for p in range(3):
                term = product(parts[p], slice(p * LANES + n * STEP, p * LANES + (n + 1) * STEP))
                total = term if total is None else total + term
            here = rests[3 * n:3 * n + 3]
            if here:
                here = [product(rest, rest_cols(0)) for rest in here]
                here += [jnp.zeros_like(here[0])] * (3 - len(here))
                total = total + jnp.concatenate(here, axis=1)
            emit(n, total)

    def lanes(n):
        return pl.ds(n * STEP if isinstance(n, int) else pl.multiple_of(n * STEP, STEP), STEP)

    def chunk(t, s, n):
        return remote(obuf.at[t, s, :, lanes(n)], xr.at[t, s, :, lanes(n)], oss.at[t, s, n], ors.at[t, s, n], across)

    def give_across(t, s, now):
        swaps[t, s].wait_recv()

        def emit(n, total):
            obuf[t, s, :, lanes(n)] = total.astype(bf16)
            if now:
                chunk(t, s, n).start()

        post(t, s, 1 - x, emit)

    def send_across(t, s):
        for n in range(LANES // STEP):
            chunk(t, s, n).start()

    def keep(t, s):
        def emit(n, total):
            own[s, :, lanes(n)] = total

        post(t, s, x, emit)

    def onward(t, s, d):
        to = lax.rem(z + d, NZ)
        return remote(zb.at[t, s, to], rz.at[t, s, z], zss.at[t, s, d], zrs.at[t, s, d], at_z(to))

    def give_back(t, s):
        @pl.loop(0, LANES // STEP)
        def _(n):
            chunk(t, s, n).wait_recv()
            total = own[s, :, lanes(n)] + xr[t, s, :, lanes(n)].astype(f32)
            zb[t, s, :, :, :, lanes(n)] = total.astype(bf16).reshape(NZ, 2, 16, STEP)

        for d in (4, 3, 5, 2, 6, 1, 7):
            onward(t, s, d).start()
        rz[t, s, z] = zb[t, s, z]

    def merge(t, s):
        pass

    def finish(t, s):
        for d in range(1, NZ):
            onward(t, s, d).wait_recv()

        for core in range(2):
            totals = []
            for e in range(2):
                total = rz[t, s, 4 * e, core].astype(f32)
                for i in range(1, 4):
                    total = total + rz[t, s, 4 * e + i, core].astype(f32)
                totals.append(total)
            added = mixed(mt[t, s, core], ms[t, s, core], jnp.concatenate(totals, axis=0))
            fresh = src[t, s, :, core].reshape(32, LANES).astype(f32) + added
            nv[t, s, core] = fresh.astype(bf16).reshape(2, 16, LANES)

    def mixing(t):
        if t == 0:
            for copy in twin_tables:
                copy.wait_recv()
        for s in range(2):
            for core, names, gains in ((c, ids, weights), (other, idt, wtt)):
                choose, scaled, _, _ = tables(names[t, s], gains[t, s])
                mt[t, s, core], ms[t, s, core] = mixer(choose, scaled)

    def prepare(s):
        behind[s].wait_recv()
        bulk[s].wait_recv()
        touched = tables(rt2[s])[3][:1]
        choose = tables(ids[1, s])[0] * (1.0 - touched)
        for half in range(2):
            base[s, half] = pack(choose, xb.at[s], half).astype(bf16)

    def pass_rows(s):
        return [go(remote(nv.at[0, s, core], nw.at[0, s, c], pss.at[1, s, i], prs.at[1, s, i], (me, twin)[i],
                          section(steps[s])))
                for i, core in enumerate((c, other))]

    def second_rows(s, arriving):
        for copy in arriving:
            copy.wait_recv()
        by_row, by_slot = mixer(tables(ids[1, s])[0], tables(rt2[s])[2])
        for half in range(2):
            rows = base[s, half].astype(f32) + mixed(by_row, by_slot, nw[0, s, half].reshape(32, LANES).astype(f32))
            pk[1, s, half] = rows.astype(bf16).reshape(2, 16, LANES)
        copy = go(remote(pk.at[1, s, other], src.at[1, s, :, c], twss.at[6 + s], twrs.at[6 + s], twin))
        src[1, s, :, c] = pk[1, s, c]
        copy.wait_recv()

    def place(names, rows, old, new):
        _, _, lone, _ = tables(names)
        touched = tn(lone.astype(bf16), jnp.ones((16, 128), bf16))[:, :1] > 0.0
        parts, rests = expand(lone)
        for half in range(2):
            fresh = rows[half].reshape(32, LANES)
            for p in range(3):
                cols = part_cols(half, p)
                new[:, cols] = jnp.where(touched, tn(parts[p], fresh), old[:, cols].astype(f32)).astype(bf16)
            cols = rest_cols(half)
            put = None
            for i in range(CAP):
                term = tn(rests[i], fresh[:, 128 * i:128 * i + 128])
                put = term if put is None else put + term
            new[:, cols] = jnp.where(touched, put, old[:, cols].astype(f32)).astype(bf16)

    def exchange_last(s):
        nw[1, s, c] = nv[1, s, c]
        return go(remote(nv.at[1, s, other], nw.at[1, s, c], twss.at[8 + s], twrs.at[8 + s], twin))

    for s in range(2):
        for copy in first_rows[s]:
            copy.wait_recv()
        dispatch(0, s)
    for t in range(2):
        relay_first(t, 0)
        relay_last(t, 0)
        if t == 0:
            for copy in local_copies:
                copy.wait()
            for copy in weight_copies:
                copy.wait_recv()
        pre(t, 0, x)
        relay_first(t, 1)
        relay_last(t, 1)
        arrived(t, 0)
        pre(t, 0, 1 - x)
        swap(t, 0)
        pre(t, 1, x)
        give_across(t, 0, True)
        keep(t, 0)
        arrived(t, 1)
        pre(t, 1, 1 - x)
        swap(t, 1)
        mixing(t)
        give_across(t, 1, True)
        give_back(t, 0)
        keep(t, 1)
        if t == 0:
            prepare(0)
        merge(t, 0)
        give_back(t, 1)
        merge(t, 1)
        if t == 0:
            prepare(1)
            finish(0, 0)
            passed = pass_rows(0)
            second_rows(0, passed)
            dispatch(1, 0)
            finish(0, 1)
            passed = pass_rows(1)
            second_rows(1, passed)
            dispatch(1, 1)
    for s, half_done in enumerate((out0, out1)):
        place(rt2[s], nw[0, s], xb.at[s], half_done)
    finish(1, 0)
    last = exchange_last(0)
    last.wait_recv()
    place(ids[1, 0], nw[1, 0], out0, out0)
    finish(1, 1)
    exchange_last(1).wait_recv()
    place(ids[1, 1], nw[1, 1], out1, out1)

    for copy in started:
        copy.wait_send()
    for t in range(2):
        for s in range(2):
            @pl.loop(0, LANES // STEP)
            def _(n):
                chunk(t, s, n).wait_send()

            for d in range(1, NZ):
                onward(t, s, d).wait_send()


def local(forward_in, grad_in, routes, gate_weights, saved_preact, gate_up, down_proj):
    bf16, f32 = jnp.bfloat16, jnp.float32
    tokens, width = forward_in.shape[1:]
    ids = jnp.transpose(routes[0], (0, 1, 3, 2))
    weights = jnp.transpose(gate_weights[0], (0, 1, 3, 2))
    stored = jnp.transpose(saved_preact[0, :, 0].reshape(2, NZ, 2, 2, CAP, 256), (0, 2, 1, 3, 4, 5))
    stored = jnp.pad(stored, ((0, 0), (0, 0), (0, 0), (0, 0), (0, 8 - CAP), (0, 0))).reshape(2, 2, 128, 256)
    vmem = pl.BlockSpec(memory_space=pltpu.VMEM)
    hbm = pl.BlockSpec(memory_space=pl.ANY)
    dma = pltpu.SemaphoreType.DMA
    out = pl.pallas_call(
        relay_kernel,
        out_shape=(jax.ShapeDtypeStruct((tokens, width), bf16),) * 2,
        in_specs=[hbm, hbm, vmem, vmem, vmem, hbm, hbm],
        out_specs=(vmem, vmem),
        scratch_shapes=[
            pltpu.VMEM((2, tokens, width), bf16),
            pltpu.VMEM((2, tokens, width), bf16),
            pltpu.VMEM((2, 8, tokens), jnp.int32),
            pltpu.VMEM((2, 8, tokens), jnp.int32),
            pltpu.VMEM((2, 2, 8, tokens), jnp.int32),
            pltpu.VMEM((2, 2, 8, tokens), f32),
            pltpu.VMEM((2, 2, 2, 2, 16, LANES), bf16),
            pltpu.VMEM((2, 2, 2, 2, 16, LANES), bf16),
            pltpu.VMEM((2, 2, 2, NZ, 2, 16, LANES), bf16),
            pltpu.VMEM((2, HALF, 256), bf16),
            pltpu.VMEM((256, HALF), bf16),
            pltpu.VMEM((2, 2, 2, 128, 256), bf16),
            pltpu.VMEM((2, 2, 128, 512), f32),
            pltpu.VMEM((2, 2, 128, 512), f32),
            pltpu.VMEM((2, 2, 128, 256), f32),
            pltpu.VMEM((2, 2, 128, 256), f32),
            pltpu.VMEM((2, 2, 256, LANES), bf16),
            pltpu.VMEM((2, 2, 256, LANES), bf16),
            pltpu.VMEM((2, 256, LANES), f32),
            pltpu.VMEM((2, 2, NZ, 2, 16, LANES), bf16),
            pltpu.VMEM((2, 2, NZ, 2, 16, LANES), bf16),
            pltpu.VMEM((2, 2, 2, 32, 32), f32),
            pltpu.VMEM((2, 2, 2, 16, 16), f32),
            pltpu.VMEM((2, 2, 2, 2, 16, LANES), bf16),
            pltpu.VMEM((2, 2, 2, 2, 16, LANES), bf16),
            pltpu.VMEM((2, 2, 32, LANES), bf16),
            dma((4,)),
            dma((3,)), dma((3,)),
            dma((2, 2)), dma((2, 2)),
            dma((2, 2, 2)), dma((2, 2, 2)),
            dma((2,)), dma((2,)),
            dma((10,)), dma((10,)),
            dma((2, 2, 8)), dma((2, 2, 8)),
            dma((2, 2, 8)), dma((2, 2, 8)),
            dma((2, 2, 3)), dma((2, 2, 3)),
            dma((2, 2, 8)), dma((2, 2, 8)),
        ],
        compiler_params=pltpu.CompilerParams(
            collective_id=0, has_side_effects=True, vmem_limit_bytes=56 * 2 ** 20),
        name="expert_relay",
    )(forward_in[0], grad_in[0], ids, weights, stored, gate_up[0, 0], down_proj[0, 0])
    return (out[0][None], out[1][None])


def solution(mesh):
    in_specs = (
        P("pp", "ep", None),
        P("pp", "ep", None),
        P("pp", None, None, "ep", None),
        P("pp", None, None, "ep", None),
        P("pp", None, "ep", None, None, None),
        P("pp", "ep", None, None),
        P("pp", "ep", None, None),
    )
    out_specs = (P("pp", "ep", None), P("pp", "ep", None))
    return jax.shard_map(local, mesh=mesh, in_specs=in_specs, out_specs=out_specs, check_vma=False)
```
